32 devices in a mesh: groups: 2 (over y), pair: 16 (over z, x, core).
Axes of the slice: x: 2, y: 2, z: 4, core: 2. Of those that a mesh axis runs over, the one named last changes fastest.
Arguments:
- amplitudes: bfloat16 [2048, 8, 4096], P(('groups', 'pair')), parts along dimension 0, may hold values from -6 to 6
- screen: int32 [2048, 8], P(('groups', 'pair')), parts along dimension 0, may hold values from 0 to 15, all different within a row; in each aligned block of 64 rows (0 to 63, 64 to 127, ...) at most 48 rows name the same one
- owner: int32 [32], P('groups'), parts along dimension 0, may hold values from 0 to 15, each once
- factors: bfloat16 [32, 2, 8, 64, 64], P(('groups', 'pair')), parts along dimension 0, may hold values from -0.4375 to 0.4375
- cycle_self: bfloat16 [2048, 64], P(('groups', 'pair')), parts along dimension 0, may hold values from -3 to 3
- cycle_prev: bfloat16 [2048, 64], P(('groups', 'pair')), parts along dimension 0, may hold values from -3 to 3
Outputs:
- residual: bfloat16 [2048, 8, 4096], P(('groups', 'pair')), parts along dimension 0
The draws below stay inside these ranges and needn't reach their ends.
There are 2 independent parts, one for each index of `groups`. The reference program is written for one: setup_inputs(seed, part) draws one part's arguments, and reference() takes and returns one part's arrays. A program takes and returns all parts, laid end to end along the dimension named above; each array names one. Nothing has to cross between parts.
Inputs may be any that keep to these rules, and one draw needn't show every extreme that they name: `screen`: each row names 8 different virtual-pair tiles. In each aligned block of 64 rows (one occupied-pair tile) no tile is named by more than 48 rows, a bound that some block reaches. A permutation: the factors of virtual-pair tile q are row owner[q] of factors.
All inputs are finite; a program needn't handle non-finite values.
Results may differ from the reference program's by a relative error of at most 0.0032.
Values may be sent and summed in bfloat16 or wider, within the bound.
A program may use at most 512 MiB of HBM per device.

```python
import math
import jax
import jax.numpy as jnp
import numpy as np
from jax import lax

VT = 64
PAIR_DEV = 64
K = 8
NAUX = 8
NPAIRS = 1024
NQ = 16
MOST = 48
N_PAIR = 16


def block_scale(key, shape, split, least, high):
    factor_of, own = 1.0, jax.random.fold_in(key, 6)
    for axis_at, parts in split:
        draws = jnp.exp(jax.random.uniform(jax.random.fold_in(own, axis_at), (parts,), jnp.float32, least / len(split), high / len(split)))
        factor_of = factor_of * jnp.repeat(draws, shape[axis_at] // parts).reshape([-1 if axis == axis_at else 1 for axis in range(len(shape))])
    return factor_of


def deal_out(stream_key, own, number, rows, amount, top, reach, slope):
    order = jax.random.permutation(stream_key, amount)
    heavy_load, common = portions_of(amount, rows * top, reach, slope, True), portions_of(amount, rows * top, reach, slope, False)
    places = jnp.arange(amount)

    def named(sizes, turn):
        used = int((sizes > 0).sum())
        fixed = max(1, used // 4)
        shifted = fixed + (places - fixed + turn * (used - fixed)) % max(1, amount - fixed)
        return jnp.zeros((amount,), jnp.int32).at[order[jnp.where(places < fixed, places, shifted)]].set(jnp.asarray(sizes, jnp.int32))

    sizes = jnp.where(number % 4 == 0, named(heavy_load, number // 4), named(common, number - number // 4 - 1))
    mixed = jax.random.permutation(jax.random.fold_in(own, 3), amount)
    source_of, sink = mixed[0:amount // 2 * 2:2], mixed[1:amount // 2 * 2:2]
    room = jnp.minimum(sizes[source_of] - 1, reach - sizes[sink]) // 2
    room = jnp.where((source_of == order[0]) | (sink == order[0]) | (sizes[sink] == 0), 0, jnp.maximum(room, 0))
    shifted = jax.random.randint(jax.random.fold_in(own, 4), (amount // 2,), 0, 1 << 20) % (room + 1)
    sizes = sizes.at[source_of].add(-shifted).at[sink].add(shifted)
    members = jnp.searchsorted(jnp.cumsum(sizes), jnp.arange(rows * top), side="right").astype(jnp.int32)
    grid = members.reshape(top, rows).T
    grid = grid[jax.random.permutation(jax.random.fold_in(own, 1), rows)]
    turn = jax.random.randint(jax.random.fold_in(own, 2), (rows, 1), 0, top)
    return jnp.take_along_axis(grid, (jnp.arange(top)[None, :] + turn) % top, axis=1)


def portions_of(number_of, total, most, skew, full):
    weights = [(1 << 20) // math.isqrt(rank ** skew) + 1 for rank in range(1, number_of + 1)]
    largest = most if full else min(most, max(-(-total // number_of), total * weights[0] // sum(weights)))
    least = 1 if total - largest >= number_of - 1 else 0
    holding, spare = [largest] + [least] * (number_of - 1), total - largest - least * (number_of - 1)
    while spare > 0:
        movable = [i for i in range(1, number_of) if holding[i] < largest] or [i for i in range(1, number_of) if holding[i] < most]
        pool, left = sum([weights[i] for i in movable]), spare
        for i in movable:
            extra = min(most - holding[i], max(1, left * weights[i] // pool), spare)
            holding[i] = holding[i] + extra
            spare = spare - extra
    return np.array(holding)


def bell_draw(own_key, shape, deviation, bound, shards=(), held_as=jnp.bfloat16):
    values = deviation * jax.random.normal(own_key, shape, jnp.float32)
    if shards:
        values = values * block_scale(own_key, shape, shards, -0.22, 0.18)
    return jnp.clip(values, -bound, bound).astype(held_as)


def setup_inputs(seed: int = 0, part: int = 0) -> dict:
    splits = jax.random.split(jax.random.key(seed), 7)
    part_keys = jax.random.split(jax.random.fold_in(splits[6], part), 7)
    amplitudes = bell_draw(part_keys[0], (NPAIRS, K, VT * VT), 1.0, 6.0, ((0, 16),))
    screen_keys = jax.random.split(jax.random.fold_in(part_keys[1], 1), NPAIRS // PAIR_DEV)
    screen_turns = jax.random.permutation(jax.random.fold_in(part_keys[1], 3), NPAIRS // PAIR_DEV)
    screen = jax.vmap(lambda own, number: deal_out(jax.random.fold_in(part_keys[1], 2), own, number, PAIR_DEV, NQ, K, MOST, 2))(screen_keys, screen_turns).reshape((NPAIRS, K))
    owner = jax.random.permutation(part_keys[2], NQ).astype(jnp.int32)
    factors = bell_draw(part_keys[3], (NQ, 2, NAUX, VT, VT), (3 * VT) ** -0.5, 0.4375, ((0, 16),))
    cycle_self = bell_draw(part_keys[4], (NPAIRS, PAIR_DEV), 0.5, 3.0, ((0, 16),))
    cycle_prev = bell_draw(part_keys[5], (NPAIRS, PAIR_DEV), 0.5, 3.0, ((0, 16),))
    return dict(amplitudes=amplitudes, screen=screen, owner=owner, factors=factors, cycle_self=cycle_self, cycle_prev=cycle_prev)


def coupled(coupling, first_ids, second_ids, second_items):
    spread = jnp.repeat(jnp.repeat(coupling.astype(jnp.float32), K, 0), K, 1)
    weights = jnp.where(first_ids[:, None] == second_ids[None, :], spread, jnp.zeros_like(spread))
    return jnp.dot(weights, second_items.astype(jnp.float32), precision=lax.Precision.HIGHEST, preferred_element_type=jnp.float32)


def reference(amplitudes, screen, owner, factors, cycle_self, cycle_prev):
    width = VT * VT
    per_tile = PAIR_DEV * K
    amps_ext = jnp.concatenate([jnp.zeros((PAIR_DEV, K, width), amplitudes.dtype), amplitudes], 0)
    screen_ext = jnp.concatenate([jnp.full((PAIR_DEV, K), -1, jnp.int32), screen.astype(jnp.int32)], 0)

    def one_tile(tile):
        start = (tile * PAIR_DEV).astype(jnp.int32)
        window = lax.dynamic_slice_in_dim(amps_ext, start, 2 * PAIR_DEV, 0)
        window_ids = lax.dynamic_slice_in_dim(screen_ext, start, 2 * PAIR_DEV, 0)
        earlier = window[:PAIR_DEV].reshape(per_tile, width)
        current = window[PAIR_DEV:].reshape(per_tile, width)
        earlier_ids = window_ids[:PAIR_DEV].reshape(per_tile)
        current_ids = window_ids[PAIR_DEV:].reshape(per_tile)
        own_coupling = lax.dynamic_slice_in_dim(cycle_self, start, PAIR_DEV, 0)
        prev_coupling = lax.dynamic_slice_in_dim(cycle_prev, start, PAIR_DEV, 0)
        cycle = coupled(own_coupling, current_ids, current_ids, current)
        cycle = cycle + coupled(prev_coupling, current_ids, earlier_ids, earlier)
        holders = owner[current_ids]
        tiles = current.reshape(per_tile, VT, VT).astype(jnp.float32)
        total = jnp.zeros((per_tile, VT, VT), jnp.float32)
        for index in range(NAUX):
            left = factors[holders, 0, index].astype(jnp.float32)
            right = factors[holders, 1, index].astype(jnp.float32)
            half = jnp.einsum("nac,ncd->nad", left, tiles, precision=lax.Precision.HIGHEST).astype(jnp.bfloat16)
            half = lax.optimization_barrier(half).astype(jnp.float32)
            total = total + jnp.einsum("nad,nbd->nab", half, right, precision=lax.Precision.HIGHEST)
        ladder = lax.optimization_barrier(total.astype(jnp.bfloat16)).astype(jnp.float32)
        summed = ladder.reshape(per_tile, width) + cycle
        return summed.astype(jnp.bfloat16).reshape(PAIR_DEV, K, width)

    result = lax.map(one_tile, jnp.arange(N_PAIR, dtype=jnp.int32))
    return result.reshape(PAIR_DEV * N_PAIR, K, width)
```

```python
import functools

import jax
import jax.numpy as jnp
from jax import lax
from jax.experimental import pallas as pl
from jax.experimental.pallas import tpu as pltpu
from jax.sharding import PartitionSpec as P

BF, F32 = jnp.bfloat16, jnp.float32


def shifted(value, axis, steps):
    count = lax.axis_size(axis)
    first, last = (max(0, -steps), min(count, count - steps))
    return lax.ppermute(value, axis, [(source, source + steps) for source in range(first, last)])


def spread_weights(coupling, first_ids, second_ids, listed):
    spread = jnp.repeat(jnp.repeat(coupling, listed, 0), listed, 1)
    return jnp.where(first_ids[:, None] == second_ids[None, :], spread, jnp.zeros_like(spread))


def ladder_kernel(
    tiles, chunks, most, vt, naux,
    owner_ref, slot_row_ref, slot_col_ref, x_ref, w_ref, f_ref,
    out_ref, g_ref, l_ref, z_ref, xt_ref, h_ref, b_ref, o_ref,
):
    step = pl.program_id(0)
    half_rows = most // 2
    pieces = vt // 2
    quads = most // 4
    items = x_ref.shape[0]
    slots = tiles * most
    lane = lax.broadcasted_iota(jnp.int32, (half_rows, 128), 1)
    low = lane < 64
    width = x_ref.shape[1]

    @pl.when(step == 0)
    def _():
        xt_ref[...] = jnp.zeros_like(xt_ref)

    @pl.when(step < chunks)
    def _():
        place = lax.broadcasted_iota(jnp.int32, (slots, items), 0)
        hot = jnp.where(place == slot_row_ref[...], 1.0, 0.0).astype(BF)
        picked = jnp.dot(hot, x_ref[...], preferred_element_type=F32)
        g_ref[:, pl.ds(pl.multiple_of(step * width, width), width)] = picked.astype(BF)

    @pl.when(jnp.logical_and(step >= chunks, step < chunks + tiles))
    def _():
        base = pl.multiple_of((step - chunks) * most, most)
        factor = f_ref[0]
        row = lax.broadcasted_iota(jnp.int32, (2 * vt, 4 * vt), 0)
        col = lax.broadcasted_iota(jnp.int32, (2 * vt, 4 * vt), 1)
        copies = jnp.where(row == vt + col % vt, 1.0, 0.0).astype(BF)
        tiled = jnp.dot(factor, copies, preferred_element_type=F32)
        part = lax.broadcasted_iota(jnp.int32, (vt, 4 * vt), 1) // vt
        for g in range(naux):
            for mi in range(4):
                b_ref[(g * 4 + mi) * vt : (g * 4 + mi + 1) * vt, :] = jnp.where(
                    part == mi, tiled[g * vt : (g + 1) * vt, :], 0.0
                ).astype(BF)
        for j in range(pieces):
            both = g_ref[pl.ds(base, most), j * 128 : (j + 1) * 128].astype(F32)
            first, second = both[:half_rows], both[half_rows:]
            z_ref[j * half_rows : (j + 1) * half_rows, :] = jnp.where(
                low, first, pltpu.roll(second, 64, 1)
            )
            z_ref[(pieces + j) * half_rows : (pieces + j + 1) * half_rows, :] = jnp.where(
                low, pltpu.roll(first, 64, 1), second
            )
        for m in range(half_rows):
            xt_ref[0:vt, m * 128 : (m + 1) * 128] = z_ref[pl.ds(m, vt, stride=half_rows), :].astype(BF)
        for k in range(quads):
            half = jnp.dot(factor, xt_ref[:, k * 256 : (k + 1) * 256], preferred_element_type=F32)
            half = half.astype(BF)
            for g in range(naux):
                h_ref[k * vt : (k + 1) * vt, g * 256 : (g + 1) * 256] = half[g * vt : (g + 1) * vt, :]
        result = jnp.dot(h_ref[...], b_ref[...], preferred_element_type=F32)
        for k in range(quads):
            for side in range(2):
                m = 2 * k + side
                o_ref[m * vt : (m + 1) * vt, :] = result[
                    k * vt : (k + 1) * vt, side * 128 : (side + 1) * 128
                ]
        for j in range(pieces):
            even = o_ref[pl.ds(j, half_rows, stride=vt), :]
            odd = o_ref[pl.ds(pieces + j, half_rows, stride=vt), :]
            first = jnp.where(low, even, pltpu.roll(odd, 64, 1))
            second = jnp.where(low, pltpu.roll(even, 64, 1), odd)
            l_ref[pl.ds(base, most), j * 128 : (j + 1) * 128] = jnp.concatenate(
                [first, second], 0
            ).astype(BF)

    @pl.when(step >= chunks + tiles)
    def _():
        at = pl.multiple_of((step - chunks - tiles) * width, width)
        place = lax.broadcasted_iota(jnp.int32, (items, slots), 1)
        hot = jnp.where(place == slot_col_ref[...], 1.0, 0.0).astype(BF)
        ladder = jnp.dot(hot, l_ref[:, pl.ds(at, width)], preferred_element_type=F32)
        out_ref[...] = ladder + jnp.dot(w_ref[...], x_ref[...], preferred_element_type=F32)


def last_kernel(part_ref, w_ref, x_ref, out_ref):
    out_ref[...] = (
        part_ref[...] + jnp.dot(w_ref[...], x_ref[...], preferred_element_type=F32)
    ).astype(BF)


def shards(amplitudes, screen, owner, factors, cycle_self, cycle_prev):
    pair_rows, listed, width = amplitudes.shape
    naux, vt = factors.shape[2], factors.shape[3]
    tiles = owner.shape[0]
    items = pair_rows * listed
    most = max(2, 3 * items // (2 * tiles))
    most = -(-most // 16) * 16
    slots = tiles * most
    chunks, wide = 8, width // 8
    x = amplitudes.reshape(items, width)
    ids = screen.reshape(items)
    earlier, earlier_ids = shifted((amplitudes, screen), "pair", 1)

    left = factors[:, 0].reshape(1, naux, vt // 2, 2, vt // 2, 2)
    left = left.transpose(0, 1, 3, 2, 5, 4).reshape(1, naux * vt, vt)
    right = factors[:, 1].transpose(0, 1, 3, 2).reshape(1, naux * vt, vt)
    packed = jnp.concatenate([left, right], 2)
    everything = lax.all_gather(packed, "pair", axis=0, tiled=True)

    same = ids[:, None] == ids[None, :]
    order = jnp.arange(items, dtype=jnp.int32)
    ahead = jnp.where(same & (order[:, None] < order[None, :]), 1, 0)
    slot = ids * most + jnp.sum(ahead, axis=0, dtype=jnp.int32)
    own_weights = spread_weights(cycle_self, ids, ids, listed)

    def x_at(s, *_):
        return (0, jnp.where(s < chunks, s, jnp.maximum(s - chunks - tiles, 0)))

    partial = pl.pallas_call(
        functools.partial(ladder_kernel, tiles, chunks, most, vt, naux),
        out_shape=jax.ShapeDtypeStruct((items, width), F32),
        grid_spec=pltpu.PrefetchScalarGridSpec(
            num_scalar_prefetch=1,
            grid=(chunks + tiles + chunks,),
            in_specs=[
                pl.BlockSpec((1, items), lambda s, o: (0, 0)),
                pl.BlockSpec((items, 1), lambda s, o: (0, 0)),
                pl.BlockSpec((items, wide), x_at),
                pl.BlockSpec((items, items), lambda s, o: (0, 0)),
                pl.BlockSpec(
                    (1, naux * vt, 2 * vt),
                    lambda s, o: (o[jnp.clip(s - chunks, 0, tiles - 1)], 0, 0),
                ),
            ],
            out_specs=pl.BlockSpec(
                (items, wide), lambda s, o: (0, jnp.maximum(s - chunks - tiles, 0))
            ),
            scratch_shapes=[
                pltpu.VMEM((slots, width), BF),
                pltpu.VMEM((slots, width), BF),
                pltpu.VMEM((vt * most // 2, 128), F32),
                pltpu.VMEM((2 * vt, most * vt), BF),
                pltpu.VMEM((most // 4 * vt, naux * 256), BF),
                pltpu.VMEM((naux * 256, 256), BF),
                pltpu.VMEM((vt * most // 2, 128), F32),
            ],
        ),
        compiler_params=pltpu.CompilerParams(vmem_limit_bytes=56 * 2**20),
        cost_estimate=pl.CostEstimate(
            flops=60 * 10**9, bytes_accessed=20 * 2**20, transcendentals=0
        ),
        name="ladder",
    )(owner, slot[None, :], slot[:, None], x, own_weights, everything)

    earlier_weights = spread_weights(cycle_prev, ids, earlier_ids.reshape(items), listed)
    residual = pl.pallas_call(
        last_kernel,
        out_shape=jax.ShapeDtypeStruct((items, width), BF),
        grid=(chunks,),
        in_specs=[
            pl.BlockSpec((items, wide), lambda s: (0, s)),
            pl.BlockSpec((items, items), lambda s: (0, 0)),
            pl.BlockSpec((items, wide), lambda s: (0, s)),
        ],
        out_specs=pl.BlockSpec((items, wide), lambda s: (0, s)),
        compiler_params=pltpu.CompilerParams(vmem_limit_bytes=32 * 2**20),
        name="cycle",
    )(partial, earlier_weights, earlier.reshape(items, width))
    return residual.reshape(pair_rows, listed, width)


def solution(mesh):
    placed = (
        P(("groups", "pair"), None, None),
        P(("groups", "pair"), None),
        P("groups"),
        P(("groups", "pair"), None, None, None, None),
        P(("groups", "pair"), None),
        P(("groups", "pair"), None),
    )
    return jax.shard_map(
        shards,
        mesh=mesh,
        in_specs=placed,
        out_specs=P(("groups", "pair"), None, None),
        check_vma=False,
    )
```

```python
import functools

import jax
import jax.numpy as jnp
from jax import lax
from jax.experimental import pallas as pl
from jax.experimental.pallas import tpu as pltpu
from jax.sharding import PartitionSpec as P

BF, F32 = jnp.bfloat16, jnp.float32


def shifted(value, axis, steps):
    count = lax.axis_size(axis)
    first, last = (max(0, -steps), min(count, count - steps))
    return lax.ppermute(value, axis, [(source, source + steps) for source in range(first, last)])


def spread_weights(coupling, first_ids, second_ids, listed):
    spread = jnp.repeat(jnp.repeat(coupling, listed, 0), listed, 1)
    return jnp.where(first_ids[:, None] == second_ids[None, :], spread, jnp.zeros_like(spread))


def spread_kernel(
    chunks, most, vt, slot_row_ref, x_ref, xt_ref, g_ref, z_ref, hot_ref
):
    step = pl.program_id(0)
    half_rows = most // 2
    pieces = vt // 2
    slots, items = hot_ref.shape
    width = x_ref.shape[1]
    low = lax.broadcasted_iota(jnp.int32, (half_rows, 128), 1) < 64

    @pl.when(step == 0)
    def _():
        place = lax.broadcasted_iota(jnp.int32, (slots, items), 0)
        hot_ref[...] = jnp.where(place == slot_row_ref[...], 1.0, 0.0).astype(BF)

    @pl.when(step < chunks)
    def _():
        picked = jnp.dot(hot_ref[...], x_ref[...], preferred_element_type=F32)
        g_ref[:, pl.ds(pl.multiple_of(step * width, width), width)] = picked.astype(BF)

    @pl.when(step >= chunks)
    def _():
        base = pl.multiple_of((step - chunks) * most, most)
        for j in range(pieces):
            both = g_ref[pl.ds(base, most), j * 128 : (j + 1) * 128].astype(F32)
            first, second = both[:half_rows], both[half_rows:]
            z_ref[j * half_rows : (j + 1) * half_rows, :] = jnp.where(
                low, first, pltpu.roll(second, 64, 1)
            )
            z_ref[(pieces + j) * half_rows : (pieces + j + 1) * half_rows, :] = jnp.where(
                low, pltpu.roll(first, 64, 1), second
            )
        for m in range(half_rows):
            xt_ref[0, :, m * 128 : (m + 1) * 128] = z_ref[
                pl.ds(m, vt, stride=half_rows), :
            ].astype(BF)


def ladder_kernel(
    most, vt, naux, owner_ref, count_ref, f_ref, xt_ref, l_ref, h_ref, b_ref, o_ref
):
    half_rows = most // 2
    pieces = vt // 2
    quads = most // 4
    pitch = vt + 8
    low = lax.broadcasted_iota(jnp.int32, (half_rows, 128), 1) < 64
    count = count_ref[pl.program_id(0)]
    row = lax.broadcasted_iota(jnp.int32, (2 * vt, 4 * vt), 0)
    col = lax.broadcasted_iota(jnp.int32, (2 * vt, 4 * vt), 1)
    copies = jnp.where(row == vt + col % vt, 1.0, 0.0).astype(BF)
    tiled = jnp.dot(f_ref[0], copies, preferred_element_type=F32)
    part = lax.broadcasted_iota(jnp.int32, (vt, 4 * vt), 1) // vt
    for g in range(naux):
        for mi in range(4):
            b_ref[(g * 4 + mi) * vt : (g * 4 + mi + 1) * vt, :] = jnp.where(
                part == mi, tiled[g * vt : (g + 1) * vt, :], 0.0
            ).astype(BF)

    def run(used):
        left = f_ref[0, :, :vt]
        for k in range(used):
            half = jnp.dot(
                left, xt_ref[0, :, k * 256 : (k + 1) * 256], preferred_element_type=F32
            ).astype(BF)
            for g in range(naux):
                h_ref[k * vt : (k + 1) * vt, g * 256 : (g + 1) * 256] = half[
                    g * vt : (g + 1) * vt, :
                ]
        result = jnp.dot(h_ref[: used * vt, :], b_ref[...], preferred_element_type=F32)
        for k in range(used):
            for side in range(2):
                m = 2 * k + side
                o_ref[m * pitch : m * pitch + vt, :] = result[
                    k * vt : (k + 1) * vt, side * 128 : (side + 1) * 128
                ]
        if used < quads:
            o_ref[2 * used * pitch :, :] = jnp.zeros((2 * (quads - used) * pitch, 128), F32)

    unit = quads // 4
    for turn in range(4):
        least = turn * unit * 4
        most_here = least + unit * 4
        fits = count <= most_here
        if turn > 0:
            fits = jnp.logical_and(fits, count > least)
        pl.when(fits)(functools.partial(run, (turn + 1) * unit))

    for j in range(pieces):
        even = o_ref[pl.ds(j, half_rows, stride=pitch), :]
        odd = o_ref[pl.ds(pieces + j, half_rows, stride=pitch), :]
        first = jnp.where(low, even, pltpu.roll(odd, 64, 1))
        second = jnp.where(low, pltpu.roll(even, 64, 1), odd)
        l_ref[:, j * 128 : (j + 1) * 128] = jnp.concatenate([first, second], 0).astype(BF)


def own_kernel(w_ref, x_ref, out_ref):
    out_ref[...] = jnp.dot(w_ref[...], x_ref[...], preferred_element_type=F32)


def last_kernel(slot_col_ref, l_ref, part_ref, v_ref, e_ref, out_ref, hot_ref):
    @pl.when(pl.program_id(0) == 0)
    def _():
        place = lax.broadcasted_iota(jnp.int32, hot_ref.shape, 1)
        hot_ref[...] = jnp.where(place == slot_col_ref[...], 1.0, 0.0).astype(BF)

    total = jnp.dot(hot_ref[...], l_ref[...], preferred_element_type=F32)
    total += part_ref[...]
    total += jnp.dot(v_ref[...], e_ref[...], preferred_element_type=F32)
    out_ref[...] = total.astype(BF)


def shards(amplitudes, screen, owner, factors, cycle_self, cycle_prev):
    pair_rows, listed, width = amplitudes.shape
    naux, vt = factors.shape[2], factors.shape[3]
    tiles = owner.shape[0]
    items = pair_rows * listed
    most = max(2, 3 * items // (2 * tiles))
    most = -(-most // 16) * 16
    slots = tiles * most
    chunks, wide = 8, width // 8
    x = amplitudes.reshape(items, width)
    ids = screen.reshape(items)
    earlier_ids = shifted(screen, "pair", 1)

    left = factors[:, 0].reshape(1, naux, vt // 2, 2, vt // 2, 2)
    left = left.transpose(0, 1, 3, 2, 5, 4).reshape(1, naux * vt, vt)
    right = factors[:, 1].transpose(0, 1, 3, 2).reshape(1, naux * vt, vt)
    packed = jnp.concatenate([left, right], 2)
    everything = lax.all_gather(packed, "pair", axis=0, tiled=True)

    same = ids[:, None] == ids[None, :]
    order = jnp.arange(items, dtype=jnp.int32)
    ahead = jnp.where(same & (order[:, None] < order[None, :]), 1, 0)
    rank = jnp.sum(ahead, axis=0, dtype=jnp.int32)
    slot = ids * most + rank % 2 * (most // 2) + rank // 2
    named = ids[:, None] == jnp.arange(tiles, dtype=jnp.int32)[None, :]
    count = jnp.sum(named, axis=0, dtype=jnp.int32)
    own_weights = spread_weights(cycle_self, ids, ids, listed)

    columns = pl.pallas_call(
        functools.partial(spread_kernel, chunks, most, vt),
        out_shape=jax.ShapeDtypeStruct((tiles, vt, most * vt), BF),
        grid=(chunks + tiles,),
        in_specs=[
            pl.BlockSpec((1, items), lambda s: (0, 0)),
            pl.BlockSpec((items, wide), lambda s: (0, jnp.minimum(s, chunks - 1))),
        ],
        out_specs=pl.BlockSpec(
            (1, vt, most * vt), lambda s: (jnp.maximum(s - chunks, 0), 0, 0)
        ),
        scratch_shapes=[
            pltpu.VMEM((slots, width), BF),
            pltpu.VMEM((vt * most // 2, 128), F32),
            pltpu.VMEM((slots, items), BF),
        ],
        compiler_params=pltpu.CompilerParams(vmem_limit_bytes=56 * 2**20),
        cost_estimate=pl.CostEstimate(
            flops=25 * 10**9, bytes_accessed=10 * 2**20, transcendentals=0
        ),
        name="spread",
    )(slot[None, :], x)

    own = pl.pallas_call(
        own_kernel,
        out_shape=jax.ShapeDtypeStruct((items, width), F32),
        grid=(chunks,),
        in_specs=[
            pl.BlockSpec((items, items), lambda s: (0, 0)),
            pl.BlockSpec((items, wide), lambda s: (0, s)),
        ],
        out_specs=pl.BlockSpec((items, wide), lambda s: (0, s)),
        compiler_params=pltpu.CompilerParams(vmem_limit_bytes=56 * 2**20),
        cost_estimate=pl.CostEstimate(
            flops=3 * 10**9, bytes_accessed=12 * 2**20, transcendentals=0
        ),
        name="own",
    )(own_weights, x)

    held, columns, own = lax.optimization_barrier((amplitudes, columns, own))
    earlier = shifted(held, "pair", 1)
    ladder = pl.pallas_call(
        functools.partial(ladder_kernel, most, vt, naux),
        out_shape=jax.ShapeDtypeStruct((slots, width), BF),
        grid_spec=pltpu.PrefetchScalarGridSpec(
            num_scalar_prefetch=2,
            grid=(tiles,),
            in_specs=[
                pl.BlockSpec((1, naux * vt, 2 * vt), lambda s, o, n: (o[s], 0, 0)),
                pl.BlockSpec((1, vt, most * vt), lambda s, o, n: (s, 0, 0)),
            ],
            out_specs=pl.BlockSpec((most, width), lambda s, o, n: (s, 0)),
            scratch_shapes=[
                pltpu.VMEM((most // 4 * vt, naux * 256), BF),
                pltpu.VMEM((naux * 256, 256), BF),
                pltpu.VMEM(((vt + 8) * most // 2, 128), F32),
            ],
        ),
        compiler_params=pltpu.CompilerParams(vmem_limit_bytes=56 * 2**20),
        cost_estimate=pl.CostEstimate(
            flops=40 * 10**9, bytes_accessed=14 * 2**20, transcendentals=0
        ),
        name="ladder",
    )(owner, count, everything, columns)

    earlier_weights = spread_weights(cycle_prev, ids, earlier_ids.reshape(items), listed)
    residual = pl.pallas_call(
        last_kernel,
        out_shape=jax.ShapeDtypeStruct((items, width), BF),
        grid=(chunks,),
        in_specs=[
            pl.BlockSpec((items, 1), lambda s: (0, 0)),
            pl.BlockSpec((slots, wide), lambda s: (0, s)),
            pl.BlockSpec((items, wide), lambda s: (0, s)),
            pl.BlockSpec((items, items), lambda s: (0, 0)),
            pl.BlockSpec((items, wide), lambda s: (0, s)),
        ],
        out_specs=pl.BlockSpec((items, wide), lambda s: (0, s)),
        scratch_shapes=[pltpu.VMEM((items, slots), BF)],
        compiler_params=pltpu.CompilerParams(vmem_limit_bytes=56 * 2**20),
        cost_estimate=pl.CostEstimate(
            flops=8 * 10**9, bytes_accessed=18 * 2**20, transcendentals=0
        ),
        name="cycle",
    )(slot[:, None], ladder, own, earlier_weights, earlier.reshape(items, width))
    return residual.reshape(pair_rows, listed, width)


def solution(mesh):
    placed = (
        P(("groups", "pair"), None, None),
        P(("groups", "pair"), None),
        P("groups"),
        P(("groups", "pair"), None, None, None, None),
        P(("groups", "pair"), None),
        P(("groups", "pair"), None),
    )
    return jax.shard_map(
        shards,
        mesh=mesh,
        in_specs=placed,
        out_specs=P(("groups", "pair"), None, None),
        check_vma=False,
    )
```

```python
import functools

import jax
import jax.numpy as jnp
from jax import lax
from jax.experimental import pallas as pl
from jax.experimental.pallas import tpu as pltpu
from jax.sharding import PartitionSpec as P

BF, F32 = jnp.bfloat16, jnp.float32


def shifted(value, axis, steps):
    count = lax.axis_size(axis)
    first, last = (max(0, -steps), min(count, count - steps))
    return lax.ppermute(value, axis, [(source, source + steps) for source in range(first, last)])


def spread_weights(coupling, first_ids, second_ids, listed):
    spread = jnp.repeat(jnp.repeat(coupling, listed, 0), listed, 1)
    return jnp.where(first_ids[:, None] == second_ids[None, :], spread, jnp.zeros_like(spread))


def spread_kernel(
    chunks, most, vt, slot_row_ref, x_ref, xt_ref, g_ref, z_ref, hot_ref
):
    step = pl.program_id(0)
    half_rows = most // 2
    pieces = vt // 2
    slots, items = hot_ref.shape
    width = x_ref.shape[1]
    low = lax.broadcasted_iota(jnp.int32, (half_rows, 128), 1) < 64

    @pl.when(step == 0)
    def _():
        place = lax.broadcasted_iota(jnp.int32, (slots, items), 0)
        hot_ref[...] = jnp.where(place == slot_row_ref[...], 1.0, 0.0).astype(BF)

    @pl.when(step < chunks)
    def _():
        picked = jnp.dot(hot_ref[...], x_ref[...], preferred_element_type=F32)
        g_ref[:, pl.ds(pl.multiple_of(step * width, width), width)] = picked.astype(BF)

    @pl.when(step >= chunks)
    def _():
        base = pl.multiple_of((step - chunks) * most, most)
        for j in range(pieces):
            both = g_ref[pl.ds(base, most), j * 128 : (j + 1) * 128].astype(F32)
            first, second = both[:half_rows], both[half_rows:]
            z_ref[j * half_rows : (j + 1) * half_rows, :] = jnp.where(
                low, first, pltpu.roll(second, 64, 1)
            )
            z_ref[(pieces + j) * half_rows : (pieces + j + 1) * half_rows, :] = jnp.where(
                low, pltpu.roll(first, 64, 1), second
            )
        for m in range(half_rows):
            xt_ref[0, :, m * 128 : (m + 1) * 128] = z_ref[
                pl.ds(m, vt, stride=half_rows), :
            ].astype(BF)


def ladder_kernel(
    most, vt, naux, owner_ref, count_ref, f_ref, xt_ref, l_ref, h_ref, b_ref, o_ref
):
    half_rows = most // 2
    pieces = vt // 2
    quads = most // 4
    pitch = vt + 8
    low = lax.broadcasted_iota(jnp.int32, (half_rows, 128), 1) < 64
    count = count_ref[pl.program_id(0)]
    @pl.when(pl.program_id(0) == 0)
    def _():
        o_ref[...] = jnp.zeros_like(o_ref)

    def run(used):
        for j in range(pieces):
            even = o_ref[pl.ds(j, half_rows, stride=pitch), :]
            odd = o_ref[pl.ds(pieces + j, half_rows, stride=pitch), :]
            first = jnp.where(low, even, pltpu.roll(odd, 64, 1))
            second = jnp.where(low, pltpu.roll(even, 64, 1), odd)
            l_ref[:, j * 128 : (j + 1) * 128] = jnp.concatenate([first, second], 0).astype(BF)
        row = lax.broadcasted_iota(jnp.int32, (2 * vt, 4 * vt), 0)
        col = lax.broadcasted_iota(jnp.int32, (2 * vt, 4 * vt), 1)
        copies = jnp.where(row == vt + col % vt, 1.0, 0.0).astype(BF)
        tiled = jnp.dot(f_ref[0], copies, preferred_element_type=F32)
        part = lax.broadcasted_iota(jnp.int32, (vt, 4 * vt), 1) // vt
        for g in range(naux):
            for mi in range(4):
                b_ref[(g * 4 + mi) * vt : (g * 4 + mi + 1) * vt, :] = jnp.where(
                    part == mi, tiled[g * vt : (g + 1) * vt, :], 0.0
                ).astype(BF)
        left = f_ref[0, :, :vt]
        for k in range(used):
            half = jnp.dot(
                left, xt_ref[0, :, k * 256 : (k + 1) * 256], preferred_element_type=F32
            ).astype(BF)
            for g in range(naux):
                h_ref[k * vt : (k + 1) * vt, g * 256 : (g + 1) * 256] = half[
                    g * vt : (g + 1) * vt, :
                ]
        result = jnp.dot(h_ref[: used * vt, :], b_ref[...], preferred_element_type=F32)
        for k in range(used):
            for side in range(2):
                m = 2 * k + side
                o_ref[m * pitch : m * pitch + vt, :] = result[
                    k * vt : (k + 1) * vt, side * 128 : (side + 1) * 128
                ]
        if used < quads:
            o_ref[2 * used * pitch :, :] = jnp.zeros((2 * (quads - used) * pitch, 128), F32)

    unit = quads // 4
    for turn in range(4):
        least = turn * unit * 4
        most_here = least + unit * 4
        fits = count <= most_here
        if turn > 0:
            fits = jnp.logical_and(fits, count > least)
        pl.when(fits)(functools.partial(run, (turn + 1) * unit))


def own_kernel(w_ref, x_ref, out_ref):
    out_ref[...] = jnp.dot(w_ref[...], x_ref[...], preferred_element_type=F32)


def last_kernel(slot_col_ref, l_ref, part_ref, v_ref, e_ref, out_ref, hot_ref):
    @pl.when(pl.program_id(0) == 0)
    def _():
        place = lax.broadcasted_iota(jnp.int32, hot_ref.shape, 1)
        hot_ref[...] = jnp.where(place == slot_col_ref[...], 1.0, 0.0).astype(BF)

    total = jnp.dot(hot_ref[...], l_ref[...], preferred_element_type=F32)
    total += part_ref[...]
    total += jnp.dot(v_ref[...], e_ref[...], preferred_element_type=F32)
    out_ref[...] = total.astype(BF)


def shards(amplitudes, screen, owner, factors, cycle_self, cycle_prev):
    pair_rows, listed, width = amplitudes.shape
    naux, vt = factors.shape[2], factors.shape[3]
    tiles = owner.shape[0]
    items = pair_rows * listed
    most = max(2, 3 * items // (2 * tiles))
    most = -(-most // 16) * 16
    slots = tiles * most
    chunks, wide = 8, width // 8
    x = amplitudes.reshape(items, width)
    ids = screen.reshape(items)
    earlier_ids = shifted(screen, "pair", 1)

    left = factors[:, 0].reshape(1, naux, vt // 2, 2, vt // 2, 2)
    left = left.transpose(0, 1, 3, 2, 5, 4).reshape(1, naux * vt, vt)
    right = factors[:, 1].transpose(0, 1, 3, 2).reshape(1, naux * vt, vt)
    packed = jnp.concatenate([left, right], 2)
    everything = lax.all_gather(packed, "pair", axis=0, tiled=True)

    same = ids[:, None] == ids[None, :]
    order = jnp.arange(items, dtype=jnp.int32)
    ahead = jnp.where(same & (order[:, None] < order[None, :]), 1, 0)
    rank = jnp.sum(ahead, axis=0, dtype=jnp.int32)
    slot = ids * most + rank % 2 * (most // 2) + rank // 2
    named = ids[:, None] == jnp.arange(tiles + 1, dtype=jnp.int32)[None, :]
    count = jnp.sum(named, axis=0, dtype=jnp.int32)
    own_weights = spread_weights(cycle_self, ids, ids, listed)

    columns = pl.pallas_call(
        functools.partial(spread_kernel, chunks, most, vt),
        out_shape=jax.ShapeDtypeStruct((tiles, vt, most * vt), BF),
        grid=(chunks + tiles,),
        in_specs=[
            pl.BlockSpec((1, items), lambda s: (0, 0)),
            pl.BlockSpec((items, wide), lambda s: (0, jnp.minimum(s, chunks - 1))),
        ],
        out_specs=pl.BlockSpec(
            (1, vt, most * vt), lambda s: (jnp.maximum(s - chunks, 0), 0, 0)
        ),
        scratch_shapes=[
            pltpu.VMEM((slots, width), BF),
            pltpu.VMEM((vt * most // 2, 128), F32),
            pltpu.VMEM((slots, items), BF),
        ],
        compiler_params=pltpu.CompilerParams(vmem_limit_bytes=56 * 2**20),
        cost_estimate=pl.CostEstimate(
            flops=25 * 10**9, bytes_accessed=10 * 2**20, transcendentals=0
        ),
        name="spread",
    )(slot[None, :], x)

    own = pl.pallas_call(
        own_kernel,
        out_shape=jax.ShapeDtypeStruct((items, width), F32),
        grid=(chunks,),
        in_specs=[
            pl.BlockSpec((items, items), lambda s: (0, 0)),
            pl.BlockSpec((items, wide), lambda s: (0, s)),
        ],
        out_specs=pl.BlockSpec((items, wide), lambda s: (0, s)),
        compiler_params=pltpu.CompilerParams(vmem_limit_bytes=56 * 2**20),
        cost_estimate=pl.CostEstimate(
            flops=3 * 10**9, bytes_accessed=12 * 2**20, transcendentals=0
        ),
        name="own",
    )(own_weights, x)

    held, columns = lax.optimization_barrier((amplitudes, columns))
    earlier = shifted(held, "pair", 1)
    ladder = pl.pallas_call(
        functools.partial(ladder_kernel, most, vt, naux),
        out_shape=jax.ShapeDtypeStruct((slots, width), BF),
        grid_spec=pltpu.PrefetchScalarGridSpec(
            num_scalar_prefetch=2,
            grid=(tiles + 1,),
            in_specs=[
                pl.BlockSpec((1, naux * vt, 2 * vt), lambda s, o, n: (o[jnp.minimum(s, tiles - 1)], 0, 0)),
                pl.BlockSpec((1, vt, most * vt), lambda s, o, n: (jnp.minimum(s, tiles - 1), 0, 0)),
            ],
            out_specs=pl.BlockSpec((most, width), lambda s, o, n: (jnp.maximum(s - 1, 0), 0)),
            scratch_shapes=[
                pltpu.VMEM((most // 4 * vt, naux * 256), BF),
                pltpu.VMEM((naux * 256, 256), BF),
                pltpu.VMEM(((vt + 8) * most // 2, 128), F32),
            ],
        ),
        compiler_params=pltpu.CompilerParams(vmem_limit_bytes=56 * 2**20),
        cost_estimate=pl.CostEstimate(
            flops=40 * 10**9, bytes_accessed=14 * 2**20, transcendentals=0
        ),
        name="ladder",
    )(owner, count, everything, columns)

    earlier_weights = spread_weights(cycle_prev, ids, earlier_ids.reshape(items), listed)
    residual = pl.pallas_call(
        last_kernel,
        out_shape=jax.ShapeDtypeStruct((items, width), BF),
        grid=(chunks // 2,),
        in_specs=[
            pl.BlockSpec((items, 1), lambda s: (0, 0)),
            pl.BlockSpec((slots, 2 * wide), lambda s: (0, s)),
            pl.BlockSpec((items, 2 * wide), lambda s: (0, s)),
            pl.BlockSpec((items, items), lambda s: (0, 0)),
            pl.BlockSpec((items, 2 * wide), lambda s: (0, s)),
        ],
        out_specs=pl.BlockSpec((items, 2 * wide), lambda s: (0, s)),
        scratch_shapes=[pltpu.VMEM((items, slots), BF)],
        compiler_params=pltpu.CompilerParams(vmem_limit_bytes=56 * 2**20),
        cost_estimate=pl.CostEstimate(
            flops=8 * 10**9, bytes_accessed=18 * 2**20, transcendentals=0
        ),
        name="cycle",
    )(slot[:, None], ladder, own, earlier_weights, earlier.reshape(items, width))
    return residual.reshape(pair_rows, listed, width)


def solution(mesh):
    placed = (
        P(("groups", "pair"), None, None),
        P(("groups", "pair"), None),
        P("groups"),
        P(("groups", "pair"), None, None, None, None),
        P(("groups", "pair"), None),
        P(("groups", "pair"), None),
    )
    return jax.shard_map(
        shards,
        mesh=mesh,
        in_specs=placed,
        out_specs=P(("groups", "pair"), None, None),
        check_vma=False,
    )
```
